512 devices in a mesh: section: 4 (over y), tok: 32 (over z, core), voc: 4 (over x).
Axes of the slice: x: 4, y: 4, z: 16, core: 2. Of those that a mesh axis runs over, the one named last changes fastest.
Arguments:
- hidden: bfloat16 [512, 4096], P(('tok', 'voc'), 'section'), may hold values from -1.4 to 1.4
- norm_gain: float32 [4096], P('section'), may hold values from 0.5 to 1.5
- value_weight: float32 [4096], P('section'), may hold values from -0.09375 to 0.09375
- head_weight: bfloat16 [98304, 4096], P(('tok', 'voc'), 'section'), may hold values from -0.3 to 0.3
- targets: int32 [512], P('section'), may hold values from 0 to 98303
- response_mask: int32 [512], P(('tok', 'voc')), may hold values 0 or 1
- loss_weight: float32 [512], P(('tok', 'voc')), may hold values from -1.5 to 1.5
- value_target: float32 [512], P(('tok', 'voc')), may hold values from -5 to 5
Outputs:
- logprobs: float32 [512], P('section')
- values: float32 [512], P(('tok', 'voc'))
- hidden_grad: bfloat16 [512, 4096], P(('tok', 'voc'), 'section')
The draws below stay inside these ranges and needn't reach their ends.
All inputs are finite; a program needn't handle non-finite values. No bound on the sum of `response_mask` on one device may be relied on, other than what follows from the above.
Results may differ from the reference program's by a relative error of at most 0.0039.
Values may be sent and summed in bfloat16 or wider, within the bound.
No kernel may reach another device: no remote copies, remote signals or barrier semaphores. Data moves between devices by JAX's collectives and lax.ppermute only.
A program may use at most 64 MiB of HBM per device.

```python
import jax
import jax.numpy as jnp
from jax import lax

D = 4096
VOCAB = 98304
TOKENS = 512


def loguniform_draw(key, shape, low_end, high_end):
    return jnp.exp(jax.random.uniform(key, shape, jnp.float32, jnp.log(low_end), jnp.log(high_end)))


def draw_hidden(key, part):
    key = jax.random.fold_in(key, 11)
    key_base, key_rows, key_cols = jax.random.split(key, 3)
    rising = 3.0 ** (0.5 * jnp.arange(D, dtype=jnp.float32) / D)
    base = jnp.clip(jax.random.normal(key_base, (TOKENS, D), jnp.float32), -4.0, 4.0)
    row_scale = loguniform_draw(key_rows, (TOKENS,), 0.01, 0.1)
    col_scale = loguniform_draw(key_cols, (D,), 0.5, 2.0) * rising
    field = base * row_scale[:, None] * col_scale[None, :]
    return field.astype(jnp.bfloat16)


def draw_head_weight(key, part):
    key = jax.random.fold_in(key, 23)
    spread = 3.0 / jnp.sqrt(jnp.float32(D))
    weights = jnp.clip(jax.random.normal(key, (VOCAB, D), jnp.float32), -4.0, 4.0) * spread
    return weights.astype(jnp.bfloat16)


def plant(result, own_key, low, top_value):
    extent = result.shape
    index_at = [jax.random.randint(jax.random.fold_in(own_key, axis), (), 0, extent[axis]) for axis in range(len(extent))]
    result = result.at[tuple(index_at)].set(low)
    longest = extent.index(max(extent))
    index_at[longest] = (index_at[longest] + 1) % extent[longest]
    return result.at[tuple(index_at)].set(top_value)


def block_levels(key, shape, cuts, smallest, high):
    level, own = 1.0, jax.random.fold_in(key, 6)
    for dim, blocks in cuts:
        heights = jnp.exp(jax.random.uniform(jax.random.fold_in(own, dim), (blocks,), jnp.float32, smallest / len(cuts), high / len(cuts)))
        level = level * jnp.repeat(heights, shape[dim] // blocks).reshape([-1 if axis == dim else 1 for axis in range(len(shape))])
    return level


def normal_values(stream_key, shape, width, most, shards=(), held_as=jnp.bfloat16):
    result = width * jax.random.normal(stream_key, shape, jnp.float32)
    if shards:
        result = result * block_levels(stream_key, shape, shards, -0.22, 0.18)
    return jnp.clip(result, -most, most).astype(held_as)


def setup_inputs(seed: int = 0) -> dict:
    streams_of = jax.random.split(jax.random.key(seed), 9)
    hidden = draw_hidden(jax.random.fold_in(streams_of[8], 71), 0)
    norm_gain = jnp.clip(1.0 + 0.1 * jax.random.normal(streams_of[1], (D,), jnp.float32), 0.5, 1.5)
    value_weight = normal_values(streams_of[2], (D,), D ** -0.5, 0.09375, ((0, 4),), jnp.float32)
    head_weight = draw_head_weight(jax.random.fold_in(streams_of[8], 71), 0)
    targets = plant(jax.random.randint(streams_of[4], (TOKENS,), 0, VOCAB), jax.random.fold_in(streams_of[4], 1), 0, VOCAB - 1).astype(jnp.int32)
    response_mask = plant((jax.random.randint(streams_of[5], (TOKENS,), 0, 4) < 3).astype(jnp.int32), jax.random.fold_in(streams_of[5], 1), 0, 1)
    loss_weight = jnp.clip(jax.random.uniform(streams_of[6], (TOKENS,), jnp.float32, -1.5, 1.5) * block_levels(streams_of[6], (TOKENS,), ((0, 128),), -0.4, 0.0), -1.5, 1.5)
    value_target = normal_values(streams_of[7], (TOKENS,), 1.0, 5.0, ((0, 128),), jnp.float32)
    return dict(hidden=hidden, norm_gain=norm_gain, value_weight=value_weight, head_weight=head_weight, targets=targets, response_mask=response_mask, loss_weight=loss_weight, value_target=value_target)


epsilon = 1e-06

def reference(hidden, norm_gain, value_weight, head_weight, targets, response_mask, loss_weight, value_target):
    hidden_rows = hidden.astype(jnp.float32)
    squares = lax.optimization_barrier(jnp.sum(hidden_rows * hidden_rows, axis=1))
    inverse = lax.rsqrt(squares / D + epsilon)
    normed = hidden_rows * inverse[:, None] * norm_gain[None, :]
    values = lax.optimization_barrier(jnp.sum(normed * value_weight[None, :], axis=1))
    rounded = normed.astype(jnp.bfloat16)
    block_rows = 128
    block_count = TOKENS // block_rows

    def one_block(index):
        first_row = (index * block_rows).astype(jnp.int32)
        chosen = lax.dynamic_slice_in_dim(rounded, first_row, block_rows, 0)
        wanted = lax.dynamic_slice_in_dim(targets, first_row, block_rows, 0)
        logits = lax.dot_general(chosen, head_weight, (((1,), (1,)), ((), ())), preferred_element_type=jnp.float32)
        highest = lax.optimization_barrier(jnp.max(logits, axis=1))
        summed_exp = lax.optimization_barrier(jnp.sum(jnp.exp(logits - highest[:, None]), axis=1))
        log_norm = highest + jnp.log(summed_exp)
        columns = lax.broadcasted_iota(jnp.int32, (1, VOCAB), 1)
        matches = columns == wanted[:, None]
        picked = lax.optimization_barrier(jnp.sum(jnp.where(matches, logits, jnp.zeros_like(logits)), axis=1))
        errors = (jnp.exp(logits - log_norm[:, None]) - matches.astype(jnp.float32)).astype(jnp.bfloat16)
        back = jnp.dot(errors, head_weight, preferred_element_type=jnp.float32)
        return (picked - log_norm, back)
    logprobs, back = lax.map(one_block, jnp.arange(block_count, dtype=jnp.int32))
    logprobs = logprobs.reshape(TOKENS)
    back = back.reshape(TOKENS, D)
    live = response_mask.astype(jnp.float32)
    cotangent = live[:, None] * (loss_weight[:, None] * back + (values - value_target)[:, None] * value_weight[None, :])
    scaled = norm_gain[None, :] * cotangent
    inner_sum = lax.optimization_barrier(jnp.sum(hidden_rows * scaled, axis=1))
    hidden_grad = inverse[:, None] * scaled - hidden_rows * (inverse * inverse * inverse * inner_sum / D)[:, None]
    return (logprobs, values, hidden_grad.astype(jnp.bfloat16))
```

```python
import jax
import jax.numpy as jnp
from jax import lax
from jax.sharding import PartitionSpec as P

epsilon = 1e-06
bf16 = jnp.bfloat16
f32 = jnp.float32


def spread(array, axis):
    size = lax.axis_size(axis)
    copies = jnp.broadcast_to(array[None], (size,) + array.shape)
    return lax.all_to_all(copies, axis, 0, 0)


def exchange(array, axis):
    return lax.all_to_all(array, axis, 0, 0)


def shards(
    hidden, norm_gain, value_weight, head_weight, targets, response_mask, loss_weight, value_target
):
    width = hidden.shape[1]
    vocab = head_weight.shape[0]
    full_width = width * lax.axis_size("section")
    hidden_rows = hidden.astype(f32)
    scaled_rows = hidden_rows * norm_gain[None, :]
    squares, raw_values = lax.psum(
        (jnp.sum(hidden_rows * hidden_rows, axis=1), jnp.sum(scaled_rows * value_weight[None, :], axis=1)),
        "section",
    )
    inverse = lax.rsqrt(squares / full_width + epsilon)
    values = inverse * raw_values
    rounded = (hidden_rows * inverse[:, None] * norm_gain[None, :]).astype(bf16)

    by_z = spread(rounded, "z")
    by_x = lax.all_gather(by_z, "x", axis=0)
    other = lax.ppermute(by_x, "core", [(0, 1), (1, 0)])
    first = lax.axis_index("core") == 0
    gathered = jnp.stack([jnp.where(first, by_x, other), jnp.where(first, other, by_x)])
    rows = gathered.reshape(2, 4, 4, 16, width).transpose(2, 0, 1, 3, 4).reshape(512, width)
    partial = lax.dot_general(
        rows, head_weight, (((1,), (1,)), ((), ())), preferred_element_type=f32
    ).astype(bf16)
    parts = exchange(partial.reshape(4, 128, vocab), "section")
    logits = jnp.sum(parts.astype(f32), axis=0)

    shard = (lax.axis_index("z") * 2 + lax.axis_index("core")) * 4 + lax.axis_index("x")
    wanted = targets.reshape(4, 2, 4, 4).transpose(1, 2, 0, 3).reshape(128)
    columns = shard * vocab + lax.broadcasted_iota(jnp.int32, (1, vocab), 1)
    matches = columns == wanted[:, None]
    local_max = jnp.max(logits, axis=1)
    local_sum = jnp.sum(jnp.exp(logits - local_max[:, None]), axis=1)
    picked = jnp.sum(jnp.where(matches, logits, jnp.zeros_like(logits)), axis=1)

    def combine(stats):
        top = jnp.max(stats[:, 0], axis=0)
        total = jnp.sum(jnp.exp(stats[:, 0] - top[None]) * stats[:, 1], axis=0)
        return jnp.stack([top, total, jnp.sum(stats[:, 2], axis=0)])

    stats = combine(spread(jnp.stack([local_max, local_sum, picked]), ("core", "x")))
    stats = combine(spread(stats, "z"))
    log_norm = stats[0] + jnp.log(stats[1])
    logprobs = (stats[2] - log_norm).reshape(2, 4, 4, 4).transpose(2, 0, 1, 3).reshape(128)
    errors = (jnp.exp(logits - log_norm[:, None]) - matches.astype(f32)).astype(bf16)
    every = lax.all_gather(errors, "section", axis=0, tiled=True)
    back = jnp.dot(every, head_weight, preferred_element_type=f32)
    back = back.astype(bf16).reshape(4, 2, 4, 16, width).transpose(1, 2, 0, 3, 4)
    back = jnp.sum(exchange(back.reshape(2, 256, width), "core").astype(f32), axis=0).astype(bf16)
    back = jnp.sum(exchange(back.reshape(4, 64, width), "x").astype(f32), axis=0).astype(bf16)
    back = jnp.sum(exchange(back.reshape(16, 4, width), "z").astype(f32), axis=0)

    live = response_mask.astype(f32)
    cotangent = live[:, None] * (
        loss_weight[:, None] * back + (values - value_target)[:, None] * value_weight[None, :]
    )
    scaled = norm_gain[None, :] * cotangent
    inner_sum = lax.psum(jnp.sum(hidden_rows * scaled, axis=1), "section")
    hidden_grad = (
        inverse[:, None] * scaled
        - hidden_rows * (inverse * inverse * inverse * inner_sum / full_width)[:, None]
    )
    return (logprobs, values, hidden_grad.astype(bf16))


def solution(mesh):
    fine = jax.sharding.Mesh(
        mesh.devices.reshape(4, 16, 2, 4), ("section", "z", "core", "x")
    )
    group = ("z", "core", "x")
    in_specs = (
        P(group, "section"),
        P("section"),
        P("section"),
        P(group, "section"),
        P("section"),
        P(group),
        P(group),
        P(group),
    )
    out_specs = (P("section"), P(group), P(group, "section"))
    return jax.shard_map(shards, mesh=fine, in_specs=in_specs, out_specs=out_specs, check_vma=False)
```

```python
import jax
import jax.numpy as jnp
from jax import lax
from jax.experimental import pallas as pl
from jax.experimental.pallas import tpu as pltpu
from jax.sharding import PartitionSpec as P

epsilon = 1e-06
bf16 = jnp.bfloat16
f32 = jnp.float32
WIDTH = 1024
VOCAB = 768
FULL = 4096
STATS = 2 * WIDTH
ROWS = STATS + 128
NT = (((1,), (1,)), ((), ()))
WAVE = 64 * 1024 * 1024 // 2


def two(value):
    high = value.astype(bf16).astype(f32)
    return [high, (value - high).astype(bf16).astype(f32)]


def three(value):
    high, low = value.astype(bf16).astype(f32), None
    return [high] + two(value - high)


def lanes(rows, columns):
    lane = lax.broadcasted_iota(jnp.int32, (rows, 128), 1)
    block = jnp.zeros((rows, 128), f32)
    for index, column in enumerate(columns):
        block = jnp.where(lane == index, column, block)
    return block


def take(block, first, last):
    lane = lax.broadcasted_iota(jnp.int32, block.shape, block.ndim - 1)
    kept = jnp.where((lane >= first) & (lane < last), block, 0.0)
    return jnp.sum(kept, axis=-1, keepdims=True)


def call(body, outs, *args, scratch=()):
    return pl.pallas_call(
        body,
        out_shape=[jax.ShapeDtypeStruct(shape, dtype) for shape, dtype in outs],
        scratch_shapes=list(scratch),
        compiler_params=pltpu.CompilerParams(vmem_limit_bytes=WAVE),
    )(*args)


def unit_of(exponent):
    return jnp.exp2(exponent)


def exponent_of(value):
    return jnp.floor(jnp.log2(jnp.maximum(value, 1e-30))) - 13.0


def digits(value):
    exponent = exponent_of(jnp.abs(value))
    scaled = value / unit_of(exponent)
    high = jnp.round(scaled)
    return [exponent, high, jnp.round((scaled - high) * 16384.0)]


def undigits(block, first):
    high, low = take(block, first + 1, first + 2), take(block, first + 2, first + 3)
    return (high + low / 16384.0) * unit_of(take(block, first, first + 1))


def project(own_ref, other_ref, gain_ref, value_ref, head_ref, out_ref):
    for half, ref in enumerate((own_ref, other_ref)):
        rows = ref[...].astype(f32)
        gained = rows * gain_ref[...]
        squares = jnp.sum(rows * rows, axis=1, keepdims=True)
        raw_values = jnp.sum(gained * value_ref[...], axis=1, keepdims=True)
        high = gained.astype(bf16)
        low = (gained - high.astype(f32)).astype(bf16)
        logits = lax.dot_general(high, head_ref[...], NT, preferred_element_type=f32)
        logits += lax.dot_general(low, head_ref[...], NT, preferred_element_type=f32)
        exponent = exponent_of(jnp.max(jnp.abs(logits), axis=1, keepdims=True))
        whole = jnp.round(logits * (1.0 / unit_of(exponent))).astype(jnp.int32).astype(jnp.int16)
        block = lanes(256, [exponent] + digits(squares) + digits(raw_values))
        block = block.astype(jnp.int32).astype(jnp.int16)
        for x in range(4):
            for s in range(4):
                source = slice(x * 64 + s * 16, x * 64 + s * 16 + 16)
                target = slice(half * 64 + x * 16, half * 64 + x * 16 + 16)
                out_ref[s, target, 0:VOCAB] = whole[source]
                out_ref[s, target, VOCAB:] = block[source]


def soften(core_ref, parts_ref, wanted_ref, out_ref, rows_ref):
    squares = raw_values = logits = 0.0
    for source in range(4):
        block = parts_ref[source, :, VOCAB:].astype(jnp.int32).astype(f32)
        whole = parts_ref[source, :, :VOCAB].astype(jnp.int32).astype(f32)
        logits = logits + whole * unit_of(take(block, 0, 1))
        squares = squares + undigits(block, 1)
        raw_values = raw_values + undigits(block, 4)
    inverse = lax.rsqrt(squares / FULL + epsilon)
    values = inverse * raw_values
    logits = logits * inverse
    column = lax.broadcasted_iota(jnp.int32, (128, VOCAB), 1)
    matches = column == wanted_ref[...]
    top = jnp.max(logits, axis=1, keepdims=True).astype(bf16).astype(f32)
    exps = jnp.exp(logits - top)
    total = jnp.sum(exps, axis=1, keepdims=True)
    first = jnp.sum(exps * logits, axis=1, keepdims=True)
    picked = jnp.sum(jnp.where(matches, logits, 0.0), axis=1, keepdims=True)
    out_ref[:, :VOCAB] = jnp.where(matches, -1.0, exps).astype(bf16)
    stats = [top] + two(total) + two(first) + two(picked) + three(inverse) + three(values)
    out_ref[:, VOCAB:] = lanes(128, stats).astype(bf16)
    pieces = lanes(128, [top] + two(total) + two(picked)).astype(bf16)
    place = lax.broadcasted_iota(jnp.int32, (128, 128), 0)
    natural = lax.broadcasted_iota(jnp.int32, (128, 128), 1)
    wanted_place = (
        ((natural // 16) % 2 ^ core_ref[0]) * 64
        + ((natural // 4) % 4) * 16
        + (natural // 32) * 4
        + natural % 4
    )
    moved = jnp.where(place == wanted_place, 1.0, 0.0).astype(bf16)
    rows_ref[...] = lax.dot_general(
        pieces, moved, (((0,), (0,)), ((), ())), preferred_element_type=f32
    )[0:16].astype(bf16)


def row_parts(top, total, picked):
    pieces = [top] + two(total) + two(picked)
    row = lax.broadcasted_iota(jnp.int32, (16, 128), 0)
    block = jnp.zeros((16, 128), f32)
    for index, piece in enumerate(pieces):
        block = jnp.where(row == index, piece, block)
    return block.astype(bf16)


def pull(exps_ref, head_ref, rows_ref, own_ref, other_ref):
    for half, ref in enumerate((own_ref, other_ref)):
        pieces = [
            exps_ref[s, half * 64 + x * 16 : half * 64 + x * 16 + 16]
            for x in range(4)
            for s in range(4)
        ]
        chosen = jnp.concatenate(pieces, axis=0)
        exps = chosen[:, :VOCAB].astype(f32)
        head = head_ref[...]
        ref[:, 0:WIDTH] = jnp.dot(
            jnp.maximum(exps, 0.0).astype(bf16), head, preferred_element_type=f32
        ).astype(bf16)
        ref[:, WIDTH:STATS] = jnp.dot(
            jnp.where(exps < 0.0, 1.0, 0.0).astype(bf16), head, preferred_element_type=f32
        ).astype(bf16)
        ref[:, STATS:ROWS] = chosen[:, VOCAB:]
        ref[:, ROWS:] = jnp.zeros((256, 128), bf16)
    other_ref[0:16, ROWS:] = rows_ref[...]


def read_rows(block):
    block = block.astype(f32)
    return block[0:1], block[1:2] + block[2:3], block[3:4] + block[4:5]


def read_lanes(block):
    block = block.astype(f32)
    return take(block, 0, 1), take(block, 1, 3), take(block, 3, 5), take(block, 5, 7)


def merge(pairs):
    top = pairs[0][0]
    for pair in pairs[1:]:
        top = jnp.maximum(top, pair[0])
    weights = [jnp.exp(pair[0] - top) for pair in pairs]
    total = weights[0] * pairs[0][1]
    for weight, pair in zip(weights[1:], pairs[1:]):
        total = total + weight * pair[1]
    return top, weights, total


def join(sources):
    stats = [read_lanes(source[1]) for source in sources]
    top, weights, total = merge(stats)
    first = sum(weight * stat[2] for weight, stat in zip(weights, stats))
    picked = sum(stat[3] for stat in stats)
    product = sum(
        weight * source[0].astype(f32) for weight, source in zip(weights, sources)
    )
    return product, top, total, first, picked


def join_rows(blocks):
    top, _, total = merge(blocks)
    return top, total, sum(block[2] for block in blocks)


def join_core(own_ref, got_ref, rows_ref, out_ref):
    product, top, total, first, picked = join(
        [(ref[:, 0:WIDTH], ref[:, STATS:ROWS]) for ref in (own_ref, got_ref)]
    )
    wanted = own_ref[:, WIDTH:STATS].astype(f32) + got_ref[:, WIDTH:STATS].astype(f32)
    block = row_parts(
        *join_rows([read_rows(rows_ref[...]), read_rows(got_ref[0:16, ROWS:])])
    )
    stats = lanes(256, [top] + two(total) + two(first) + two(picked)).astype(bf16)
    product, wanted = product.astype(bf16), wanted.astype(bf16)
    for x in range(4):
        out_ref[x, :, 0:WIDTH] = product[x * 64 : x * 64 + 64]
        out_ref[x, :, WIDTH:STATS] = wanted[x * 64 : x * 64 + 64]
        out_ref[x, :, STATS:ROWS] = stats[x * 64 : x * 64 + 64]
        out_ref[x, 0:16, ROWS:] = block
        out_ref[x, 16:64, ROWS:] = jnp.zeros((48, 128), bf16)


def join_x(got_ref, out_ref):
    product, top, total, first, picked = join(
        [(got_ref[k, :, 0:WIDTH], got_ref[k, :, STATS:ROWS]) for k in range(4)]
    )
    top_row, total_row, picked_row = join_rows(
        [read_rows(got_ref[k, 0:16, ROWS:]) for k in range(4)]
    )
    stats = lanes(64, [top] + two(total) + two(first) + two(picked))
    pieces = [top_row] + two(total_row) + two(picked_row)
    row = lax.broadcasted_iota(jnp.int32, (4, 128), 0)
    left = jnp.zeros((4, 128), f32)
    for index in range(4):
        left = jnp.where(row == index, pieces[index], left)
    right = jnp.where(row == 0, pieces[4], 0.0)
    wanted = sum(got_ref[k, :, WIDTH:STATS].astype(f32) for k in range(4))
    for z in range(16):
        some = slice(z * 4, z * 4 + 4)
        out_ref[z, :, 0:WIDTH] = product[some].astype(bf16)
        out_ref[z, :, WIDTH : 2 * WIDTH] = wanted[some].astype(bf16)
        out_ref[z, :, 2 * WIDTH : 2 * WIDTH + 128] = stats[some].astype(bf16)
        out_ref[z, :, 2 * WIDTH + 128 : 2 * WIDTH + 256] = left.astype(bf16)
        out_ref[z, :, 2 * WIDTH + 256 :] = right.astype(bf16)


def finish(
    got_ref, own_ref, hidden_ref, gain_ref, value_ref, token_ref, grad_ref, logprobs_ref
):
    product, top, total, first, picked = join(
        [
            (got_ref[k, :, 0:WIDTH], got_ref[k, :, 2 * WIDTH : 2 * WIDTH + 128])
            for k in range(16)
        ]
    )
    wanted = sum(got_ref[k, :, WIDTH : 2 * WIDTH].astype(f32) for k in range(16))
    log_norm = top + jnp.log(total)
    back = product / total + (jnp.exp(picked - log_norm) - 1.0) * wanted
    own = own_ref[...].astype(f32)
    inverse = take(own, 7, 10)
    values = take(own, 10, 13)
    token = token_ref[...]
    live, weight, value_target = token[:, 0:1], token[:, 1:2], token[:, 2:3]
    value_error = values - value_target
    cotangent = live * (weight * back + value_error * value_ref[...])
    inner = live * (weight * (first / total - picked) + value_error * values)
    rows = hidden_ref[...].astype(f32)
    grad_ref[...] = (
        inverse * gain_ref[...] * cotangent - rows * (inverse * inverse * inner / FULL)
    ).astype(bf16)
    blocks = []
    for k in range(16):
        left = got_ref[k, :, 2 * WIDTH + 128 : 2 * WIDTH + 256].astype(f32)
        right = got_ref[k, :, 2 * WIDTH + 256 :].astype(f32)
        blocks.append((left[0:1], left[1:2] + left[2:3], left[3:4] + right[0:1]))
    top_row, total_row, picked_row = join_rows(blocks)
    logprobs_ref[...] = picked_row - (top_row + jnp.log(total_row))


def spread(array, axis):
    size = lax.axis_size(axis)
    copies = jnp.broadcast_to(array[None], (size,) + array.shape)
    return lax.all_to_all(copies, axis, 0, 0)


def shards(
    hidden, norm_gain, value_weight, head_weight, targets, response_mask, loss_weight, value_target
):
    core = lax.axis_index("core")
    z, x = lax.axis_index("z"), lax.axis_index("x")
    shard = (z * 2 + core) * 4 + x
    gain, value_row = norm_gain[None, :], value_weight[None, :]
    swap = [(0, 1), (1, 0)]

    by_z = spread(hidden, "z")
    own = lax.all_gather(by_z, "x", axis=0).reshape(256, WIDTH)
    other = lax.ppermute(own, "core", swap)
    (sent,) = call(
        project, [((4, 128, VOCAB + 128), jnp.int16)], own, other, gain, value_row, head_weight
    )
    parts = lax.all_to_all(sent, "section", 0, 0)

    block = targets.reshape(4, 2, 4, 4).transpose(1, 2, 0, 3)
    block = jnp.where(core == 0, block, block[::-1]).reshape(128, 1) - shard * VOCAB
    exps, rows = pl.pallas_call(
        soften,
        out_shape=[
            jax.ShapeDtypeStruct((128, VOCAB + 128), bf16),
            jax.ShapeDtypeStruct((16, 128), bf16),
        ],
        in_specs=[
            pl.BlockSpec(memory_space=pltpu.SMEM),
            pl.BlockSpec(memory_space=pltpu.VMEM),
            pl.BlockSpec(memory_space=pltpu.VMEM),
        ],
        compiler_params=pltpu.CompilerParams(vmem_limit_bytes=WAVE),
    )(core.astype(jnp.int32).reshape(1), parts, block)
    every = lax.all_gather(exps, "section", axis=0)
    half = ((256, 2 * WIDTH + 256), bf16)
    mine, theirs = call(pull, [half, half], every, head_weight, rows)
    own_stats = lax.dynamic_slice(mine, (x * 64 + z * 4, STATS), (4, 128))
    got = lax.ppermute(theirs, "core", swap)
    (sent,) = call(join_core, [((4, 64, 2 * WIDTH + 256), bf16)], mine, got, rows)
    got = lax.all_to_all(sent, "x", 0, 0)
    (sent,) = call(join_x, [((16, 4, 2 * WIDTH + 384), bf16)], got)
    got = lax.all_to_all(sent, "z", 0, 0)
    token = jnp.stack([response_mask.astype(f32), loss_weight, value_target], axis=1)
    grad, logprobs = call(
        finish,
        [((4, WIDTH), bf16), ((1, 128), f32)],
        got,
        own_stats,
        hidden,
        gain,
        value_row,
        token,
    )
    values = jnp.sum(own_stats[:, 10:13].astype(f32), axis=1)
    return (logprobs.reshape(128), values, grad)


def solution(mesh):
    fine = jax.sharding.Mesh(
        mesh.devices.reshape(4, 16, 2, 4), ("section", "z", "core", "x")
    )
    group = ("z", "core", "x")
    in_specs = (
        P(group, "section"),
        P("section"),
        P("section"),
        P(group, "section"),
        P("section"),
        P(group),
        P(group),
        P(group),
    )
    out_specs = (P("section"), P(group), P(group, "section"))
    return jax.shard_map(shards, mesh=fine, in_specs=in_specs, out_specs=out_specs, check_vma=False)
```

```python
import jax
import jax.numpy as jnp
from jax import lax
from jax.experimental import pallas as pl
from jax.experimental.pallas import tpu as pltpu
from jax.sharding import PartitionSpec as P

epsilon = 1e-06
bf16 = jnp.bfloat16
f32 = jnp.float32
WIDTH = 1024
VOCAB = 768
FULL = 4096
STATS = 2 * WIDTH
ROWS = STATS + 128
NT = (((1,), (1,)), ((), ()))
SCOPED = 32 * 1024 * 1024


def two(value):
    high = value.astype(bf16).astype(f32)
    return [high, (value - high).astype(bf16).astype(f32)]


def three(value):
    high, low = value.astype(bf16).astype(f32), None
    return [high] + two(value - high)


def lanes(rows, columns):
    lane = lax.broadcasted_iota(jnp.int32, (rows, 128), 1)
    block = jnp.zeros((rows, 128), f32)
    for index, column in enumerate(columns):
        block = jnp.where(lane == index, column, block)
    return block


def take(block, first, last):
    lane = lax.broadcasted_iota(jnp.int32, block.shape, block.ndim - 1)
    kept = jnp.where((lane >= first) & (lane < last), block, 0.0)
    return jnp.sum(kept, axis=-1, keepdims=True)


def call(body, outs, *args, scratch=()):
    return pl.pallas_call(
        body,
        out_shape=[jax.ShapeDtypeStruct(shape, dtype) for shape, dtype in outs],
        scratch_shapes=list(scratch),
        compiler_params=pltpu.CompilerParams(vmem_limit_bytes=SCOPED),
    )(*args)


def unit_of(exponent):
    return jnp.exp2(exponent)


def exponent_of(value):
    return jnp.floor(jnp.log2(jnp.maximum(value, 1e-30))) - 13.0


def digits(value):
    exponent = exponent_of(jnp.abs(value))
    scaled = value / unit_of(exponent)
    high = jnp.round(scaled)
    return [exponent, high, jnp.round((scaled - high) * 16384.0)]


def undigits(block, first):
    high, low = take(block, first + 1, first + 2), take(block, first + 2, first + 3)
    return (high + low / 16384.0) * unit_of(take(block, first, first + 1))


def encode(ref, gain_ref, value_ref, head_ref):
    rows = ref[...].astype(f32)
    gained = rows * gain_ref[...]
    squares = jnp.sum(rows * rows, axis=1, keepdims=True)
    raw_values = jnp.sum(gained * value_ref[...], axis=1, keepdims=True)
    high = gained.astype(bf16)
    low = (gained - high.astype(f32)).astype(bf16)
    logits = lax.dot_general(high, head_ref[...], NT, preferred_element_type=f32)
    logits += lax.dot_general(low, head_ref[...], NT, preferred_element_type=f32)
    exponent = exponent_of(jnp.max(jnp.abs(logits), axis=1, keepdims=True))
    whole = jnp.round(logits * (1.0 / unit_of(exponent))).astype(jnp.int32).astype(jnp.int16)
    block = lanes(256, [exponent] + digits(squares) + digits(raw_values))
    return whole, block.astype(jnp.int32).astype(jnp.int16)


def project_own(own_ref, gain_ref, value_ref, head_ref, out_ref):
    out_ref[:, :VOCAB], out_ref[:, VOCAB:] = encode(own_ref, gain_ref, value_ref, head_ref)


def project(first_ref, other_ref, gain_ref, value_ref, head_ref, out_ref):
    whole, block = encode(other_ref, gain_ref, value_ref, head_ref)
    for x in range(4):
        for s in range(4):
            source = slice(x * 64 + s * 16, x * 64 + s * 16 + 16)
            out_ref[s, x * 16 : x * 16 + 16] = first_ref[source]
            out_ref[s, 64 + x * 16 : 64 + x * 16 + 16, :VOCAB] = whole[source]
            out_ref[s, 64 + x * 16 : 64 + x * 16 + 16, VOCAB:] = block[source]


def soften(core_ref, parts_ref, wanted_ref, out_ref, rows_ref):
    squares = raw_values = logits = 0.0
    for source in range(4):
        block = parts_ref[source, :, VOCAB:].astype(jnp.int32).astype(f32)
        whole = parts_ref[source, :, :VOCAB].astype(jnp.int32).astype(f32)
        logits = logits + whole * unit_of(take(block, 0, 1))
        squares = squares + undigits(block, 1)
        raw_values = raw_values + undigits(block, 4)
    inverse = lax.rsqrt(squares / FULL + epsilon)
    values = inverse * raw_values
    logits = logits * inverse
    column = lax.broadcasted_iota(jnp.int32, (128, VOCAB), 1)
    matches = column == wanted_ref[...]
    top = jnp.max(logits, axis=1, keepdims=True).astype(bf16).astype(f32)
    exps = jnp.exp(logits - top)
    total = jnp.sum(exps, axis=1, keepdims=True)
    first = jnp.sum(exps * logits, axis=1, keepdims=True)
    picked = jnp.sum(jnp.where(matches, logits, 0.0), axis=1, keepdims=True)
    out_ref[:, :VOCAB] = jnp.where(matches, -1.0, exps).astype(bf16)
    stats = [top] + two(total) + two(first) + two(picked) + three(inverse) + three(values)
    out_ref[:, VOCAB:] = lanes(128, stats).astype(bf16)
    pieces = lanes(128, [top] + two(total) + two(picked)).astype(bf16)
    place = lax.broadcasted_iota(jnp.int32, (128, 128), 0)
    natural = lax.broadcasted_iota(jnp.int32, (128, 128), 1)
    wanted_place = (
        ((natural // 16) % 2 ^ core_ref[0]) * 64
        + ((natural // 4) % 4) * 16
        + (natural // 32) * 4
        + natural % 4
    )
    moved = jnp.where(place == wanted_place, 1.0, 0.0).astype(bf16)
    rows_ref[...] = lax.dot_general(
        pieces, moved, (((0,), (0,)), ((), ())), preferred_element_type=f32
    )[0:16].astype(bf16)


def row_parts(top, total, picked):
    pieces = [top] + two(total) + two(picked)
    row = lax.broadcasted_iota(jnp.int32, (16, 128), 0)
    block = jnp.zeros((16, 128), f32)
    for index, piece in enumerate(pieces):
        block = jnp.where(row == index, piece, block)
    return block.astype(bf16)


def pull(half, exps_ref, head_ref, out_ref):
    pieces = [
        exps_ref[s, half * 64 + x * 16 : half * 64 + x * 16 + 16]
        for x in range(4)
        for s in range(4)
    ]
    chosen = jnp.concatenate(pieces, axis=0)
    exps = chosen[:, :VOCAB].astype(f32)
    head = head_ref[...]
    out_ref[:, 0:WIDTH] = jnp.dot(
        jnp.maximum(exps, 0.0).astype(bf16), head, preferred_element_type=f32
    ).astype(bf16)
    out_ref[:, WIDTH:STATS] = jnp.dot(
        jnp.where(exps < 0.0, 1.0, 0.0).astype(bf16), head, preferred_element_type=f32
    ).astype(bf16)
    out_ref[:, STATS:ROWS] = chosen[:, VOCAB:]


def pull_own(exps_ref, head_ref, out_ref):
    pull(0, exps_ref, head_ref, out_ref)


def pull_other(exps_ref, head_ref, rows_ref, out_ref):
    pull(1, exps_ref, head_ref, out_ref)
    out_ref[0:16, ROWS:] = rows_ref[...]
    out_ref[16:, ROWS:] = jnp.zeros((240, 128), bf16)


def read_rows(block):
    block = block.astype(f32)
    return block[0:1], block[1:2] + block[2:3], block[3:4] + block[4:5]


def read_lanes(block):
    block = block.astype(f32)
    return take(block, 0, 1), take(block, 1, 3), take(block, 3, 5), take(block, 5, 7)


def merge(pairs):
    top = pairs[0][0]
    for pair in pairs[1:]:
        top = jnp.maximum(top, pair[0])
    weights = [jnp.exp(pair[0] - top) for pair in pairs]
    total = weights[0] * pairs[0][1]
    for weight, pair in zip(weights[1:], pairs[1:]):
        total = total + weight * pair[1]
    return top, weights, total


def join(sources):
    stats = [read_lanes(source[1]) for source in sources]
    top, weights, total = merge(stats)
    first = sum(weight * stat[2] for weight, stat in zip(weights, stats))
    picked = sum(stat[3] for stat in stats)
    product = sum(
        weight * source[0].astype(f32) for weight, source in zip(weights, sources)
    )
    return product, top, total, first, picked


def join_rows(blocks):
    top, _, total = merge(blocks)
    return top, total, sum(block[2] for block in blocks)


def join_core(own_ref, got_ref, rows_ref, out_ref):
    product, top, total, first, picked = join(
        [(ref[:, 0:WIDTH], ref[:, STATS:ROWS]) for ref in (own_ref, got_ref)]
    )
    wanted = own_ref[:, WIDTH:STATS].astype(f32) + got_ref[:, WIDTH:STATS].astype(f32)
    block = row_parts(
        *join_rows([read_rows(rows_ref[...]), read_rows(got_ref[0:16, ROWS:])])
    )
    stats = lanes(256, [top] + two(total) + two(first) + two(picked)).astype(bf16)
    product, wanted = product.astype(bf16), wanted.astype(bf16)
    for x in range(4):
        out_ref[x, :, 0:WIDTH] = product[x * 64 : x * 64 + 64]
        out_ref[x, :, WIDTH:STATS] = wanted[x * 64 : x * 64 + 64]
        out_ref[x, :, STATS:ROWS] = stats[x * 64 : x * 64 + 64]
        out_ref[x, 0:16, ROWS:] = block
        out_ref[x, 16:64, ROWS:] = jnp.zeros((48, 128), bf16)


def join_x(got_ref, out_ref):
    product, top, total, first, picked = join(
        [(got_ref[k, :, 0:WIDTH], got_ref[k, :, STATS:ROWS]) for k in range(4)]
    )
    top_row, total_row, picked_row = join_rows(
        [read_rows(got_ref[k, 0:16, ROWS:]) for k in range(4)]
    )
    stats = lanes(64, [top] + two(total) + two(first) + two(picked))
    pieces = [top_row] + two(total_row) + two(picked_row)
    row = lax.broadcasted_iota(jnp.int32, (4, 128), 0)
    left = jnp.zeros((4, 128), f32)
    for index in range(4):
        left = jnp.where(row == index, pieces[index], left)
    right = jnp.where(row == 0, pieces[4], 0.0)
    wanted = sum(got_ref[k, :, WIDTH:STATS].astype(f32) for k in range(4))
    for z in range(16):
        some = slice(z * 4, z * 4 + 4)
        out_ref[z, :, 0:WIDTH] = product[some].astype(bf16)
        out_ref[z, :, WIDTH : 2 * WIDTH] = wanted[some].astype(bf16)
        out_ref[z, :, 2 * WIDTH : 2 * WIDTH + 128] = stats[some].astype(bf16)
        out_ref[z, :, 2 * WIDTH + 128 : 2 * WIDTH + 256] = left.astype(bf16)
        out_ref[z, :, 2 * WIDTH + 256 :] = right.astype(bf16)


def finish(
    got_ref, own_ref, hidden_ref, gain_ref, value_ref, token_ref, grad_ref, logprobs_ref
):
    product, top, total, first, picked = join(
        [
            (got_ref[k, :, 0:WIDTH], got_ref[k, :, 2 * WIDTH : 2 * WIDTH + 128])
            for k in range(16)
        ]
    )
    wanted = sum(got_ref[k, :, WIDTH : 2 * WIDTH].astype(f32) for k in range(16))
    log_norm = top + jnp.log(total)
    back = product / total + (jnp.exp(picked - log_norm) - 1.0) * wanted
    own = own_ref[...].astype(f32)
    inverse = take(own, 7, 10)
    values = take(own, 10, 13)
    token = token_ref[...]
    live, weight, value_target = token[:, 0:1], token[:, 1:2], token[:, 2:3]
    value_error = values - value_target
    cotangent = live * (weight * back + value_error * value_ref[...])
    inner = live * (weight * (first / total - picked) + value_error * values)
    rows = hidden_ref[...].astype(f32)
    grad_ref[...] = (
        inverse * gain_ref[...] * cotangent - rows * (inverse * inverse * inner / FULL)
    ).astype(bf16)
    blocks = []
    for k in range(16):
        left = got_ref[k, :, 2 * WIDTH + 128 : 2 * WIDTH + 256].astype(f32)
        right = got_ref[k, :, 2 * WIDTH + 256 :].astype(f32)
        blocks.append((left[0:1], left[1:2] + left[2:3], left[3:4] + right[0:1]))
    top_row, total_row, picked_row = join_rows(blocks)
    logprobs_ref[...] = picked_row - (top_row + jnp.log(total_row))


def spread(array, axis):
    size = lax.axis_size(axis)
    copies = jnp.broadcast_to(array[None], (size,) + array.shape)
    return lax.all_to_all(copies, axis, 0, 0)


def shards(
    hidden, norm_gain, value_weight, head_weight, targets, response_mask, loss_weight, value_target
):
    core = lax.axis_index("core")
    z, x = lax.axis_index("z"), lax.axis_index("x")
    shard = (z * 2 + core) * 4 + x
    gain, value_row = norm_gain[None, :], value_weight[None, :]
    swap = [(0, 1), (1, 0)]

    by_z = spread(hidden, "z")
    own = lax.all_gather(by_z, "x", axis=0).reshape(256, WIDTH)
    other = lax.ppermute(own, "core", swap)
    coded = (256, VOCAB + 128)
    (first,) = call(project_own, [(coded, jnp.int16)], own, gain, value_row, head_weight)
    (sent,) = call(
        project,
        [((4, 128, VOCAB + 128), jnp.int16)],
        first,
        other,
        gain,
        value_row,
        head_weight,
    )
    parts = lax.all_to_all(sent, "section", 0, 0)

    block = targets.reshape(4, 2, 4, 4).transpose(1, 2, 0, 3)
    block = jnp.where(core == 0, block, block[::-1]).reshape(128, 1) - shard * VOCAB
    exps, rows = pl.pallas_call(
        soften,
        out_shape=[
            jax.ShapeDtypeStruct((128, VOCAB + 128), bf16),
            jax.ShapeDtypeStruct((16, 128), bf16),
        ],
        in_specs=[
            pl.BlockSpec(memory_space=pltpu.SMEM),
            pl.BlockSpec(memory_space=pltpu.VMEM),
            pl.BlockSpec(memory_space=pltpu.VMEM),
        ],
        compiler_params=pltpu.CompilerParams(vmem_limit_bytes=SCOPED),
    )(core.astype(jnp.int32).reshape(1), parts, block)
    every = lax.all_gather(exps, "section", axis=0)
    (theirs,) = call(pull_other, [((256, ROWS + 128), bf16)], every, head_weight, rows)
    got = lax.ppermute(theirs, "core", swap)
    (mine,) = call(pull_own, [((256, ROWS), bf16)], every, head_weight)
    own_stats = lax.dynamic_slice(mine, (x * 64 + z * 4, STATS), (4, 128))
    (sent,) = call(join_core, [((4, 64, 2 * WIDTH + 256), bf16)], mine, got, rows)
    got = lax.all_to_all(sent, "x", 0, 0)
    (sent,) = call(join_x, [((16, 4, 2 * WIDTH + 384), bf16)], got)
    got = lax.all_to_all(sent, "z", 0, 0)
    token = jnp.stack([response_mask.astype(f32), loss_weight, value_target], axis=1)
    grad, logprobs = call(
        finish,
        [((4, WIDTH), bf16), ((1, 128), f32)],
        got,
        own_stats,
        hidden,
        gain,
        value_row,
        token,
    )
    values = jnp.sum(own_stats[:, 10:13].astype(f32), axis=1)
    return (logprobs.reshape(128), values, grad)


def solution(mesh):
    fine = jax.sharding.Mesh(
        mesh.devices.reshape(4, 16, 2, 4), ("section", "z", "core", "x")
    )
    group = ("z", "core", "x")
    in_specs = (
        P(group, "section"),
        P("section"),
        P("section"),
        P(group, "section"),
        P("section"),
        P(group),
        P(group),
        P(group),
    )
    out_specs = (P("section"), P(group), P(group, "section"))
    return jax.shard_map(shards, mesh=fine, in_specs=in_specs, out_specs=out_specs, check_vma=False)
```

```python
import jax
import jax.numpy as jnp
from jax import lax
from jax.experimental import pallas as pl
from jax.experimental.pallas import tpu as pltpu
from jax.sharding import PartitionSpec as P

epsilon = 1e-06
bf16 = jnp.bfloat16
f32 = jnp.float32
WIDTH = 1024
VOCAB = 768
PAIR = 2 * VOCAB
FULL = 4096
CODED = PAIR + 128
STATS = 2 * WIDTH
ROWS = STATS + 128
NT = (((1,), (1,)), ((), ()))
SCOPED = 32 * 1024 * 1024


def two(value):
    high = value.astype(bf16).astype(f32)
    return [high, (value - high).astype(bf16).astype(f32)]


def three(value):
    high, low = value.astype(bf16).astype(f32), None
    return [high] + two(value - high)


def lanes(rows, columns):
    lane = lax.broadcasted_iota(jnp.int32, (rows, 128), 1)
    block = jnp.zeros((rows, 128), f32)
    for index, column in enumerate(columns):
        block = jnp.where(lane == index, column, block)
    return block


def take(block, first, last):
    lane = lax.broadcasted_iota(jnp.int32, block.shape, block.ndim - 1)
    kept = jnp.where((lane >= first) & (lane < last), block, 0.0)
    return jnp.sum(kept, axis=-1, keepdims=True)


def call(body, outs, *args, scratch=()):
    return pl.pallas_call(
        body,
        out_shape=[jax.ShapeDtypeStruct(shape, dtype) for shape, dtype in outs],
        scratch_shapes=list(scratch),
        compiler_params=pltpu.CompilerParams(vmem_limit_bytes=SCOPED),
    )(*args)


def unit_of(exponent):
    return jnp.exp2(exponent)


def exponent_of(value):
    return jnp.floor(jnp.log2(jnp.maximum(value, 1e-30))) - 13.0


def digits(value):
    exponent = exponent_of(jnp.abs(value))
    scaled = value / unit_of(exponent)
    high = jnp.round(scaled)
    return [exponent, high, jnp.round((scaled - high) * 16384.0)]


def undigits(block, first):
    high, low = take(block, first + 1, first + 2), take(block, first + 2, first + 3)
    return (high + low / 16384.0) * unit_of(take(block, first, first + 1))


def project(own_ref, gain_ref, value_ref, near_ref, far_ref, out_ref):
    rows = own_ref[...].astype(f32)
    gained = rows * gain_ref[...]
    squares = jnp.sum(rows * rows, axis=1, keepdims=True)
    raw_values = jnp.sum(gained * value_ref[...], axis=1, keepdims=True)
    high = gained.astype(bf16)
    low = (gained - high.astype(f32)).astype(bf16)
    logits = []
    for ref in (near_ref, far_ref):
        part = lax.dot_general(high, ref[...], NT, preferred_element_type=f32)
        logits.append(part + lax.dot_general(low, ref[...], NT, preferred_element_type=f32))
    largest = [jnp.max(jnp.abs(part), axis=1, keepdims=True) for part in logits]
    exponent = exponent_of(jnp.maximum(*largest))
    scale = 1.0 / unit_of(exponent)
    pieces = [jnp.round(part * scale) for part in logits]
    pieces.append(lanes(256, [exponent] + digits(squares) + digits(raw_values)))
    for index, piece in enumerate(pieces):
        piece = piece.astype(jnp.int32).astype(jnp.int16)
        columns = slice(index * VOCAB, min((index + 1) * VOCAB, CODED))
        for x in range(4):
            for s in range(4):
                source = slice(x * 64 + s * 16, x * 64 + s * 16 + 16)
                out_ref[s, x * 16 : x * 16 + 16, columns] = piece[source]


def soften(core_ref, parts_ref, wanted_ref, out_ref, rows_ref):
    squares = raw_values = logits = 0.0
    for source in range(4):
        block = parts_ref[source, :, PAIR:].astype(jnp.int32).astype(f32)
        whole = parts_ref[source, :, :PAIR].astype(jnp.int32).astype(f32)
        logits = logits + whole * unit_of(take(block, 0, 1))
        squares = squares + undigits(block, 1)
        raw_values = raw_values + undigits(block, 4)
    inverse = lax.rsqrt(squares / FULL + epsilon)
    values = inverse * raw_values
    logits = logits * inverse
    column = lax.broadcasted_iota(jnp.int32, (64, PAIR), 1)
    matches = column == wanted_ref[...]
    top = jnp.max(logits, axis=1, keepdims=True).astype(bf16).astype(f32)
    exps = jnp.exp(logits - top)
    total = jnp.sum(exps, axis=1, keepdims=True)
    first = jnp.sum(exps * logits, axis=1, keepdims=True)
    picked = jnp.sum(jnp.where(matches, logits, 0.0), axis=1, keepdims=True)
    out_ref[:, :PAIR] = jnp.where(matches, -1.0, exps).astype(bf16)
    stats = [top] + two(total) + two(first) + two(picked) + three(inverse) + three(values)
    out_ref[:, PAIR:] = lanes(64, stats).astype(bf16)
    pieces = lanes(64, [top] + two(total) + two(picked)).astype(bf16)
    place = lax.broadcasted_iota(jnp.int32, (64, 128), 0)
    natural = lax.broadcasted_iota(jnp.int32, (64, 128), 1)
    wanted_place = ((natural // 4) % 4) * 16 + (natural // 32) * 4 + natural % 4
    mine = (natural // 16) % 2 == core_ref[0]
    moved = jnp.where((place == wanted_place) & mine, 1.0, 0.0).astype(bf16)
    rows_ref[...] = lax.dot_general(
        pieces, moved, (((0,), (0,)), ((), ())), preferred_element_type=f32
    )[0:16].astype(bf16)


def pull(exps_ref, near_ref, far_ref, rows_ref, got_ref, out_ref):
    pieces = [
        exps_ref[s, x * 16 : x * 16 + 16] for x in range(4) for s in range(4)
    ]
    chosen = jnp.concatenate(pieces, axis=0)
    product = wanted = 0.0
    for index, ref in enumerate((near_ref, far_ref)):
        exps = chosen[:, index * VOCAB : (index + 1) * VOCAB].astype(f32)
        head = ref[...]
        product += jnp.dot(
            jnp.maximum(exps, 0.0).astype(bf16), head, preferred_element_type=f32
        )
        wanted += jnp.dot(
            jnp.where(exps < 0.0, 1.0, 0.0).astype(bf16), head, preferred_element_type=f32
        )
    product, wanted = product.astype(bf16), wanted.astype(bf16)
    rows = (rows_ref[...].astype(f32) + got_ref[...].astype(f32)).astype(bf16)
    for x in range(4):
        some = slice(x * 64, x * 64 + 64)
        out_ref[x, :, 0:WIDTH] = product[some]
        out_ref[x, :, WIDTH:STATS] = wanted[some]
        out_ref[x, :, STATS:ROWS] = chosen[some, PAIR:]
        out_ref[x, 0:16, ROWS:] = rows
        out_ref[x, 16:64, ROWS:] = jnp.zeros((48, 128), bf16)


def read_rows(block):
    block = block.astype(f32)
    return block[0:1], block[1:2] + block[2:3], block[3:4] + block[4:5]


def read_lanes(block):
    block = block.astype(f32)
    return take(block, 0, 1), take(block, 1, 3), take(block, 3, 5), take(block, 5, 7)


def merge(pairs):
    top = pairs[0][0]
    for pair in pairs[1:]:
        top = jnp.maximum(top, pair[0])
    weights = [jnp.exp(pair[0] - top) for pair in pairs]
    total = weights[0] * pairs[0][1]
    for weight, pair in zip(weights[1:], pairs[1:]):
        total = total + weight * pair[1]
    return top, weights, total


def join(sources):
    stats = [read_lanes(source[1]) for source in sources]
    top, weights, total = merge(stats)
    first = sum(weight * stat[2] for weight, stat in zip(weights, stats))
    picked = sum(stat[3] for stat in stats)
    product = sum(
        weight * source[0].astype(f32) for weight, source in zip(weights, sources)
    )
    return product, top, total, first, picked


def join_rows(blocks):
    top, _, total = merge(blocks)
    return top, total, sum(block[2] for block in blocks)


def join_x(got_ref, out_ref):
    product, top, total, first, picked = join(
        [(got_ref[k, :, 0:WIDTH], got_ref[k, :, STATS:ROWS]) for k in range(4)]
    )
    top_row, total_row, picked_row = join_rows(
        [read_rows(got_ref[k, 0:16, ROWS:]) for k in range(4)]
    )
    stats = lanes(64, [top] + two(total) + two(first) + two(picked))
    pieces = [top_row] + two(total_row) + two(picked_row)
    row = lax.broadcasted_iota(jnp.int32, (4, 128), 0)
    left = jnp.zeros((4, 128), f32)
    for index in range(4):
        left = jnp.where(row == index, pieces[index], left)
    right = jnp.where(row == 0, pieces[4], 0.0)
    wanted = sum(got_ref[k, :, WIDTH:STATS].astype(f32) for k in range(4))
    for z in range(16):
        some = slice(z * 4, z * 4 + 4)
        out_ref[z, :, 0:WIDTH] = product[some].astype(bf16)
        out_ref[z, :, WIDTH : 2 * WIDTH] = wanted[some].astype(bf16)
        out_ref[z, :, 2 * WIDTH : 2 * WIDTH + 128] = stats[some].astype(bf16)
        out_ref[z, :, 2 * WIDTH + 128 : 2 * WIDTH + 256] = left.astype(bf16)
        out_ref[z, :, 2 * WIDTH + 256 :] = right.astype(bf16)


def finish(
    got_ref, own_ref, hidden_ref, gain_ref, value_ref, token_ref, grad_ref, logprobs_ref
):
    product, top, total, first, picked = join(
        [
            (got_ref[k, :, 0:WIDTH], got_ref[k, :, 2 * WIDTH : 2 * WIDTH + 128])
            for k in range(16)
        ]
    )
    wanted = sum(got_ref[k, :, WIDTH : 2 * WIDTH].astype(f32) for k in range(16))
    log_norm = top + jnp.log(total)
    back = product / total + (jnp.exp(picked - log_norm) - 1.0) * wanted
    own = own_ref[...].astype(f32)
    inverse = take(own, 7, 10)
    values = take(own, 10, 13)
    token = token_ref[...]
    live, weight, value_target = token[:, 0:1], token[:, 1:2], token[:, 2:3]
    value_error = values - value_target
    cotangent = live * (weight * back + value_error * value_ref[...])
    inner = live * (weight * (first / total - picked) + value_error * values)
    rows = hidden_ref[...].astype(f32)
    grad_ref[...] = (
        inverse * gain_ref[...] * cotangent - rows * (inverse * inverse * inner / FULL)
    ).astype(bf16)
    blocks = []
    for k in range(16):
        left = got_ref[k, :, 2 * WIDTH + 128 : 2 * WIDTH + 256].astype(f32)
        right = got_ref[k, :, 2 * WIDTH + 256 :].astype(f32)
        blocks.append((left[0:1], left[1:2] + left[2:3], left[3:4] + right[0:1]))
    top_row, total_row, picked_row = join_rows(blocks)
    logprobs_ref[...] = picked_row - (top_row + jnp.log(total_row))


def spread(array, axis):
    size = lax.axis_size(axis)
    copies = jnp.broadcast_to(array[None], (size,) + array.shape)
    return lax.all_to_all(copies, axis, 0, 0)


def shards(
    hidden, norm_gain, value_weight, head_weight, targets, response_mask, loss_weight, value_target
):
    core = lax.axis_index("core")
    z, x = lax.axis_index("z"), lax.axis_index("x")
    near = (z * 2 + core) * 4 + x
    far = (z * 2 + 1 - core) * 4 + x
    gain, value_row = norm_gain[None, :], value_weight[None, :]
    swap = [(0, 1), (1, 0)]

    far_weight = lax.ppermute(head_weight, "core", swap)
    by_z = spread(hidden, "z")
    own = lax.all_gather(by_z.reshape(64, WIDTH), "x", axis=0, tiled=True)
    (sent,) = call(
        project,
        [((4, 64, CODED), jnp.int16)],
        own,
        gain,
        value_row,
        head_weight,
        far_weight,
    )
    parts = lax.all_to_all(sent, "section", 0, 0)

    block = targets.reshape(4, 2, 4, 4).transpose(1, 2, 0, 3).reshape(2, 64)
    block = jnp.where(core == 0, block[0], block[1])
    in_near, in_far = block - near * VOCAB, block - far * VOCAB
    place = jnp.where((in_near >= 0) & (in_near < VOCAB), in_near, -1)
    place = jnp.where((in_far >= 0) & (in_far < VOCAB), in_far + VOCAB, place)
    exps, rows = pl.pallas_call(
        soften,
        out_shape=[
            jax.ShapeDtypeStruct((64, CODED), bf16),
            jax.ShapeDtypeStruct((16, 128), bf16),
        ],
        in_specs=[
            pl.BlockSpec(memory_space=pltpu.SMEM),
            pl.BlockSpec(memory_space=pltpu.VMEM),
            pl.BlockSpec(memory_space=pltpu.VMEM),
        ],
        compiler_params=pltpu.CompilerParams(vmem_limit_bytes=SCOPED),
    )(core.astype(jnp.int32).reshape(1), parts, place.reshape(64, 1))
    got_rows = lax.ppermute(rows, "core", swap)
    every = lax.all_gather(exps, "section", axis=0)
    (sent,) = call(
        pull,
        [((4, 64, ROWS + 128), bf16)],
        every,
        head_weight,
        far_weight,
        rows,
        got_rows,
    )
    own_stats = lax.dynamic_slice(every, (z // 4, x * 16 + (z % 4) * 4, PAIR), (1, 4, 128))[0]
    got = lax.all_to_all(sent, "x", 0, 0)
    (sent,) = call(join_x, [((16, 4, 2 * WIDTH + 384), bf16)], got)
    got = lax.all_to_all(sent, "z", 0, 0)
    token = jnp.stack([response_mask.astype(f32), loss_weight, value_target], axis=1)
    grad, logprobs = call(
        finish,
        [((4, WIDTH), bf16), ((1, 128), f32)],
        got,
        own_stats,
        hidden,
        gain,
        value_row,
        token,
    )
    values = jnp.sum(own_stats[:, 10:13].astype(f32), axis=1)
    return (logprobs.reshape(128), values, grad)


def solution(mesh):
    fine = jax.sharding.Mesh(
        mesh.devices.reshape(4, 16, 2, 4), ("section", "z", "core", "x")
    )
    group = ("z", "core", "x")
    in_specs = (
        P(group, "section"),
        P("section"),
        P("section"),
        P(group, "section"),
        P("section"),
        P(group),
        P(group),
        P(group),
    )
    out_specs = (P("section"), P(group), P(group, "section"))
    return jax.shard_map(shards, mesh=fine, in_specs=in_specs, out_specs=out_specs, check_vma=False)
```

```python
import jax
import jax.numpy as jnp
from jax import lax
from jax.experimental import pallas as pl
from jax.experimental.pallas import tpu as pltpu
from jax.sharding import PartitionSpec as P

epsilon = 1e-06
bf16 = jnp.bfloat16
f32 = jnp.float32
WIDTH = 1024
VOCAB = 768
PAIR = 2 * VOCAB
PIECES = 4
PARKED = 18432
FULL = 4096
CODED = PAIR + 128
STATS = 2 * WIDTH
ROWS = STATS + 128
NT = (((1,), (1,)), ((), ()))
SCOPED = 32 * 1024 * 1024


def two(value):
    high = value.astype(bf16).astype(f32)
    return [high, (value - high).astype(bf16).astype(f32)]


def three(value):
    high, low = value.astype(bf16).astype(f32), None
    return [high] + two(value - high)


def lanes(rows, columns):
    lane = lax.broadcasted_iota(jnp.int32, (rows, 128), 1)
    block = jnp.zeros((rows, 128), f32)
    for index, column in enumerate(columns):
        block = jnp.where(lane == index, column, block)
    return block


def take(block, first, last):
    lane = lax.broadcasted_iota(jnp.int32, block.shape, block.ndim - 1)
    kept = jnp.where((lane >= first) & (lane < last), block, 0.0)
    return jnp.sum(kept, axis=-1, keepdims=True)


def call(body, outs, *args, parked=None):
    scratch = []
    if parked is not None:
        scratch = [pltpu.VMEM((VOCAB, WIDTH), bf16), pltpu.SemaphoreType.DMA((PIECES,))]
    return pl.pallas_call(
        body,
        out_shape=[jax.ShapeDtypeStruct(shape, dtype) for shape, dtype in outs],
        in_specs=[
            pl.BlockSpec(memory_space=pl.ANY if index == parked else pltpu.VMEM)
            for index in range(len(args))
        ],
        scratch_shapes=scratch,
        compiler_params=pltpu.CompilerParams(vmem_limit_bytes=SCOPED),
    )(*args)


def unit_of(exponent):
    return jnp.exp2(exponent)


def exponent_of(value):
    return jnp.floor(jnp.log2(jnp.maximum(value, 1e-30))) - 13.0


def digits(value):
    exponent = exponent_of(jnp.abs(value))
    scaled = value / unit_of(exponent)
    high = jnp.round(scaled)
    return [exponent, high, jnp.round((scaled - high) * 16384.0)]


def undigits(block, first):
    high, low = take(block, first + 1, first + 2), take(block, first + 2, first + 3)
    return (high + low / 16384.0) * unit_of(take(block, first, first + 1))


def pieces_of(source, target, arrived):
    copies = []
    for index in range(PIECES):
        rows = pl.ds(index * (VOCAB // PIECES), VOCAB // PIECES)
        copies.append(
            pltpu.make_async_copy(source.at[rows], target.at[rows], arrived.at[index])
        )
    for copy in copies:
        copy.start()
    return copies


def park(far_ref, out_ref, arrived):
    for copy in pieces_of(far_ref, out_ref, arrived):
        copy.wait()


def project(own_ref, gain_ref, value_ref, near_ref, far_ref, out_ref, far_held, arrived):
    copies = pieces_of(far_ref, far_held, arrived)
    rows = own_ref[...].astype(f32)
    gained = rows * gain_ref[...]
    squares = jnp.sum(rows * rows, axis=1, keepdims=True)
    raw_values = jnp.sum(gained * value_ref[...], axis=1, keepdims=True)
    high = gained.astype(bf16)
    low = (gained - high.astype(f32)).astype(bf16)
    logits = []
    for ref in (near_ref, far_held):
        if ref is far_held:
            for copy in copies:
                copy.wait()
        part = lax.dot_general(high, ref[...], NT, preferred_element_type=f32)
        logits.append(part + lax.dot_general(low, ref[...], NT, preferred_element_type=f32))
    largest = [jnp.max(jnp.abs(part), axis=1, keepdims=True) for part in logits]
    exponent = exponent_of(jnp.maximum(*largest))
    scale = 1.0 / unit_of(exponent)
    pieces = [jnp.round(part * scale) for part in logits]
    pieces.append(lanes(256, [exponent] + digits(squares) + digits(raw_values)))
    for index, piece in enumerate(pieces):
        piece = piece.astype(jnp.int32).astype(jnp.int16)
        columns = slice(index * VOCAB, min((index + 1) * VOCAB, CODED))
        for x in range(4):
            for s in range(4):
                source = slice(x * 64 + s * 16, x * 64 + s * 16 + 16)
                out_ref[s, x * 16 : x * 16 + 16, columns] = piece[source]


def soften(core_ref, parts_ref, wanted_ref, out_ref, rows_ref):
    squares = raw_values = logits = 0.0
    for source in range(4):
        block = parts_ref[source, :, PAIR:].astype(jnp.int32).astype(f32)
        whole = parts_ref[source, :, :PAIR].astype(jnp.int32).astype(f32)
        logits = logits + whole * unit_of(take(block, 0, 1))
        squares = squares + undigits(block, 1)
        raw_values = raw_values + undigits(block, 4)
    inverse = lax.rsqrt(squares / FULL + epsilon)
    values = inverse * raw_values
    logits = logits * inverse
    column = lax.broadcasted_iota(jnp.int32, (64, PAIR), 1)
    matches = column == wanted_ref[...]
    top = jnp.max(logits, axis=1, keepdims=True).astype(bf16).astype(f32)
    exps = jnp.exp(logits - top)
    total = jnp.sum(exps, axis=1, keepdims=True)
    first = jnp.sum(exps * logits, axis=1, keepdims=True)
    picked = jnp.sum(jnp.where(matches, logits, 0.0), axis=1, keepdims=True)
    out_ref[:, :PAIR] = jnp.where(matches, -1.0, exps).astype(bf16)
    stats = [top] + two(total) + two(first) + two(picked) + three(inverse) + three(values)
    out_ref[:, PAIR:] = lanes(64, stats).astype(bf16)
    pieces = lanes(64, [top] + two(total) + two(picked)).astype(bf16)
    place = lax.broadcasted_iota(jnp.int32, (64, 128), 0)
    natural = lax.broadcasted_iota(jnp.int32, (64, 128), 1)
    wanted_place = ((natural // 4) % 4) * 16 + (natural // 32) * 4 + natural % 4
    mine = (natural // 16) % 2 == core_ref[0]
    moved = jnp.where((place == wanted_place) & mine, 1.0, 0.0).astype(bf16)
    rows_ref[...] = lax.dot_general(
        pieces, moved, (((0,), (0,)), ((), ())), preferred_element_type=f32
    )[0:16].astype(bf16)


def pull(exps_ref, near_ref, far_ref, rows_ref, got_ref, out_ref, far_held, arrived):
    copies = pieces_of(far_ref, far_held, arrived)
    pieces = [
        exps_ref[s, x * 16 : x * 16 + 16] for x in range(4) for s in range(4)
    ]
    chosen = jnp.concatenate(pieces, axis=0)
    product = wanted = 0.0
    for index, ref in enumerate((near_ref, far_held)):
        if ref is far_held:
            for copy in copies:
                copy.wait()
        exps = chosen[:, index * VOCAB : (index + 1) * VOCAB].astype(f32)
        head = ref[...]
        product += jnp.dot(
            jnp.maximum(exps, 0.0).astype(bf16), head, preferred_element_type=f32
        )
        wanted += jnp.dot(
            jnp.where(exps < 0.0, 1.0, 0.0).astype(bf16), head, preferred_element_type=f32
        )
    product, wanted = product.astype(bf16), wanted.astype(bf16)
    rows = (rows_ref[...].astype(f32) + got_ref[...].astype(f32)).astype(bf16)
    for x in range(4):
        some = slice(x * 64, x * 64 + 64)
        out_ref[x, :, 0:WIDTH] = product[some]
        out_ref[x, :, WIDTH:STATS] = wanted[some]
        out_ref[x, :, STATS:ROWS] = chosen[some, PAIR:]
        out_ref[x, 0:16, ROWS:] = rows
        out_ref[x, 16:64, ROWS:] = jnp.zeros((48, 128), bf16)


def read_rows(block):
    block = block.astype(f32)
    return block[0:1], block[1:2] + block[2:3], block[3:4] + block[4:5]


def read_lanes(block):
    block = block.astype(f32)
    return take(block, 0, 1), take(block, 1, 3), take(block, 3, 5), take(block, 5, 7)


def merge(pairs):
    top = pairs[0][0]
    for pair in pairs[1:]:
        top = jnp.maximum(top, pair[0])
    weights = [jnp.exp(pair[0] - top) for pair in pairs]
    total = weights[0] * pairs[0][1]
    for weight, pair in zip(weights[1:], pairs[1:]):
        total = total + weight * pair[1]
    return top, weights, total


def join(sources):
    stats = [read_lanes(source[1]) for source in sources]
    top, weights, total = merge(stats)
    first = sum(weight * stat[2] for weight, stat in zip(weights, stats))
    picked = sum(stat[3] for stat in stats)
    product = sum(
        weight * source[0].astype(f32) for weight, source in zip(weights, sources)
    )
    return product, top, total, first, picked


def join_rows(blocks):
    top, _, total = merge(blocks)
    return top, total, sum(block[2] for block in blocks)


def join_x(got_ref, out_ref):
    product, top, total, first, picked = join(
        [(got_ref[k, :, 0:WIDTH], got_ref[k, :, STATS:ROWS]) for k in range(4)]
    )
    top_row, total_row, picked_row = join_rows(
        [read_rows(got_ref[k, 0:16, ROWS:]) for k in range(4)]
    )
    stats = lanes(64, [top] + two(total) + two(first) + two(picked))
    pieces = two(top_row + jnp.log(total_row)) + two(picked_row)
    row = lax.broadcasted_iota(jnp.int32, (4, 128), 0)
    block = jnp.zeros((4, 128), f32)
    for index in range(4):
        block = jnp.where(row == index, pieces[index], block)
    wanted = sum(got_ref[k, :, WIDTH:STATS].astype(f32) for k in range(4))
    for z in range(16):
        some = slice(z * 4, z * 4 + 4)
        out_ref[z, :, 0:WIDTH] = product[some].astype(bf16)
        out_ref[z, :, WIDTH : 2 * WIDTH] = wanted[some].astype(bf16)
        out_ref[z, :, 2 * WIDTH : 2 * WIDTH + 128] = stats[some].astype(bf16)
        out_ref[z, :, ROWS:] = block.astype(bf16)


def finish(
    got_ref, own_ref, hidden_ref, gain_ref, value_ref, token_ref, grad_ref, logprobs_ref
):
    product, top, total, first, picked = join(
        [
            (got_ref[k, :, 0:WIDTH], got_ref[k, :, 2 * WIDTH : 2 * WIDTH + 128])
            for k in range(16)
        ]
    )
    wanted = sum(got_ref[k, :, WIDTH : 2 * WIDTH].astype(f32) for k in range(16))
    log_norm = top + jnp.log(total)
    back = product / total + (jnp.exp(picked - log_norm) - 1.0) * wanted
    own = own_ref[...].astype(f32)
    inverse = take(own, 7, 10)
    values = take(own, 10, 13)
    token = token_ref[...]
    live, weight, value_target = token[:, 0:1], token[:, 1:2], token[:, 2:3]
    value_error = values - value_target
    cotangent = live * (weight * back + value_error * value_ref[...])
    inner = live * (weight * (first / total - picked) + value_error * values)
    rows = hidden_ref[...].astype(f32)
    grad_ref[...] = (
        inverse * gain_ref[...] * cotangent - rows * (inverse * inverse * inner / FULL)
    ).astype(bf16)
    blocks = []
    for k in range(16):
        block = got_ref[k, :, ROWS:].astype(f32)
        blocks.append((block[0:1] + block[1:2], 1.0, block[2:3] + block[3:4]))
    top_row, total_row, picked_row = join_rows(blocks)
    logprobs_ref[...] = picked_row - (top_row + jnp.log(total_row))


def spread(array, axis):
    size = lax.axis_size(axis)
    copies = jnp.broadcast_to(array[None], (size,) + array.shape)
    return lax.all_to_all(copies, axis, 0, 0)


def shards(
    hidden, norm_gain, value_weight, head_weight, targets, response_mask, loss_weight, value_target
):
    core = lax.axis_index("core")
    z, x = lax.axis_index("z"), lax.axis_index("x")
    near = (z * 2 + core) * 4 + x
    far = (z * 2 + 1 - core) * 4 + x
    gain, value_row = norm_gain[None, :], value_weight[None, :]
    swap = [(0, 1), (1, 0)]

    far_weight = lax.ppermute(head_weight, "core", swap)
    far_weight = pl.pallas_call(
        park,
        out_shape=jax.ShapeDtypeStruct((PARKED, WIDTH), bf16),
        in_specs=[pl.BlockSpec(memory_space=pltpu.VMEM)],
        out_specs=pl.BlockSpec(memory_space=pl.ANY),
        scratch_shapes=[pltpu.SemaphoreType.DMA((PIECES,))],
        compiler_params=pltpu.CompilerParams(vmem_limit_bytes=SCOPED),
    )(far_weight)
    by_z = spread(hidden, "z")
    by_z, far_weight = lax.optimization_barrier((by_z, far_weight))
    own = lax.all_gather(by_z.reshape(64, WIDTH), "x", axis=0, tiled=True)
    (sent,) = call(
        project,
        [((4, 64, CODED), jnp.int16)],
        own,
        gain,
        value_row,
        head_weight,
        far_weight,
        parked=4,
    )
    parts = lax.all_to_all(sent, "section", 0, 0)

    block = targets.reshape(4, 2, 4, 4).transpose(1, 2, 0, 3).reshape(2, 64)
    block = jnp.where(core == 0, block[0], block[1])
    in_near, in_far = block - near * VOCAB, block - far * VOCAB
    place = jnp.where((in_near >= 0) & (in_near < VOCAB), in_near, -1)
    place = jnp.where((in_far >= 0) & (in_far < VOCAB), in_far + VOCAB, place)
    exps, rows = pl.pallas_call(
        soften,
        out_shape=[
            jax.ShapeDtypeStruct((64, CODED), bf16),
            jax.ShapeDtypeStruct((16, 128), bf16),
        ],
        in_specs=[
            pl.BlockSpec(memory_space=pltpu.SMEM),
            pl.BlockSpec(memory_space=pltpu.VMEM),
            pl.BlockSpec(memory_space=pltpu.VMEM),
        ],
        compiler_params=pltpu.CompilerParams(vmem_limit_bytes=SCOPED),
    )(core.astype(jnp.int32).reshape(1), parts, place.reshape(64, 1))
    got_rows = lax.ppermute(rows, "core", swap)
    every = lax.all_gather(exps, "section", axis=0)
    (sent,) = call(
        pull,
        [((4, 64, ROWS + 128), bf16)],
        every,
        head_weight,
        far_weight,
        rows,
        got_rows,
        parked=2,
    )
    own_stats = lax.dynamic_slice(every, (z // 4, x * 16 + (z % 4) * 4, PAIR), (1, 4, 128))[0]
    got = lax.all_to_all(sent, "x", 0, 0)
    (sent,) = call(join_x, [((16, 4, ROWS + 128), bf16)], got)
    got = lax.all_to_all(sent, "z", 0, 0)
    token = jnp.stack([response_mask.astype(f32), loss_weight, value_target], axis=1)
    grad, logprobs = call(
        finish,
        [((4, WIDTH), bf16), ((1, 128), f32)],
        got,
        own_stats,
        hidden,
        gain,
        value_row,
        token,
    )
    values = jnp.sum(own_stats[:, 10:13].astype(f32), axis=1)
    return (logprobs.reshape(128), values, grad)


def solution(mesh):
    fine = jax.sharding.Mesh(
        mesh.devices.reshape(4, 16, 2, 4), ("section", "z", "core", "x")
    )
    group = ("z", "core", "x")
    in_specs = (
        P(group, "section"),
        P("section"),
        P("section"),
        P(group, "section"),
        P("section"),
        P(group),
        P(group),
        P(group),
    )
    out_specs = (P("section"), P(group), P(group, "section"))
    return jax.shard_map(shards, mesh=fine, in_specs=in_specs, out_specs=out_specs, check_vma=False)
```

```python
import jax
import jax.numpy as jnp
from jax import lax
from jax.experimental import pallas as pl
from jax.experimental.pallas import tpu as pltpu
from jax.sharding import PartitionSpec as P

epsilon = 1e-06
bf16 = jnp.bfloat16
f32 = jnp.float32
WIDTH = 1024
VOCAB = 768
PAIR = 2 * VOCAB
PIECES = 3
PIECE = VOCAB // PIECES
PARKED = 18432
FULL = 4096
CODED = PAIR + 128
STATS = 2 * WIDTH
ROWS = STATS + 128
NT = (((1,), (1,)), ((), ()))
SCOPED = 32 * 1024 * 1024


def two(value):
    high = value.astype(bf16).astype(f32)
    return [high, (value - high).astype(bf16).astype(f32)]


def three(value):
    high, low = value.astype(bf16).astype(f32), None
    return [high] + two(value - high)


def lanes(rows, columns):
    lane = lax.broadcasted_iota(jnp.int32, (rows, 128), 1)
    block = jnp.zeros((rows, 128), f32)
    for index, column in enumerate(columns):
        block = jnp.where(lane == index, column, block)
    return block


def take(block, first, last):
    lane = lax.broadcasted_iota(jnp.int32, block.shape, block.ndim - 1)
    kept = jnp.where((lane >= first) & (lane < last), block, 0.0)
    return jnp.sum(kept, axis=-1, keepdims=True)


def call(body, outs, *args, parked=None):
    scratch = []
    if parked is not None:
        scratch = [pltpu.VMEM((VOCAB, WIDTH), bf16), pltpu.SemaphoreType.DMA((PIECES,))]
    return pl.pallas_call(
        body,
        out_shape=[jax.ShapeDtypeStruct(shape, dtype) for shape, dtype in outs],
        in_specs=[
            pl.BlockSpec(memory_space=pl.ANY if index == parked else pltpu.VMEM)
            for index in range(len(args))
        ],
        scratch_shapes=scratch,
        compiler_params=pltpu.CompilerParams(vmem_limit_bytes=SCOPED),
    )(*args)


def unit_of(exponent):
    return jnp.exp2(exponent)


def exponent_of(value):
    return jnp.floor(jnp.log2(jnp.maximum(value, 1e-30))) - 13.0


def digits(value):
    exponent = exponent_of(jnp.abs(value))
    scaled = value / unit_of(exponent)
    high = jnp.round(scaled)
    return [exponent, high, jnp.round((scaled - high) * 16384.0)]


def undigits(block, first):
    high, low = take(block, first + 1, first + 2), take(block, first + 2, first + 3)
    return (high + low / 16384.0) * unit_of(take(block, first, first + 1))


def pieces_of(source, target, arrived):
    copies = []
    for index in range(PIECES):
        rows = pl.ds(index * PIECE, PIECE)
        copies.append(
            pltpu.make_async_copy(source.at[rows], target.at[rows], arrived.at[index])
        )
    for copy in copies:
        copy.start()
    return copies


def heads_of(near_ref, far_held, copies):
    yield near_ref[...]
    for index, copy in enumerate(copies):
        copy.wait()
        yield far_held[index * PIECE : (index + 1) * PIECE]


def park(upper_ref, lower_ref, out_ref, arrived):
    half = VOCAB // 2
    copies = [
        pltpu.make_async_copy(upper_ref, out_ref.at[0:half], arrived.at[0]),
        pltpu.make_async_copy(lower_ref, out_ref.at[half:VOCAB], arrived.at[1]),
    ]
    for copy in copies:
        copy.start()
    for copy in copies:
        copy.wait()


def project(own_ref, gain_ref, value_ref, near_ref, far_ref, out_ref, far_held, arrived):
    copies = pieces_of(far_ref, far_held, arrived)
    rows = own_ref[...].astype(f32)
    gained = rows * gain_ref[...]
    squares = jnp.sum(rows * rows, axis=1, keepdims=True)
    raw_values = jnp.sum(gained * value_ref[...], axis=1, keepdims=True)
    high = gained.astype(bf16)
    low = (gained - high.astype(f32)).astype(bf16)
    logits = []
    for ref in (near_ref, far_held):
        if ref is far_held:
            for copy in copies:
                copy.wait()
        part = lax.dot_general(high, ref[...], NT, preferred_element_type=f32)
        logits.append(part + lax.dot_general(low, ref[...], NT, preferred_element_type=f32))
    largest = [jnp.max(jnp.abs(part), axis=1, keepdims=True) for part in logits]
    exponent = exponent_of(jnp.maximum(*largest))
    scale = 1.0 / unit_of(exponent)
    pieces = [jnp.round(part * scale) for part in logits]
    pieces.append(lanes(256, [exponent] + digits(squares) + digits(raw_values)))
    start = 0
    for piece in pieces:
        piece = piece.astype(jnp.int32).astype(jnp.int16)
        columns = slice(start, start + piece.shape[1])
        start += piece.shape[1]
        for x in range(4):
            for s in range(4):
                source = slice(x * 64 + s * 16, x * 64 + s * 16 + 16)
                out_ref[s, x * 16 : x * 16 + 16, columns] = piece[source]


def soften(core_ref, parts_ref, wanted_ref, out_ref, rows_ref):
    squares = raw_values = logits = 0.0
    for source in range(4):
        block = parts_ref[source, :, PAIR:].astype(jnp.int32).astype(f32)
        whole = parts_ref[source, :, :PAIR].astype(jnp.int32).astype(f32)
        logits = logits + whole * unit_of(take(block, 0, 1))
        squares = squares + undigits(block, 1)
        raw_values = raw_values + undigits(block, 4)
    inverse = lax.rsqrt(squares / FULL + epsilon)
    values = inverse * raw_values
    logits = logits * inverse
    column = lax.broadcasted_iota(jnp.int32, (64, PAIR), 1)
    matches = column == wanted_ref[...]
    top = jnp.max(logits, axis=1, keepdims=True).astype(bf16).astype(f32)
    exps = jnp.exp(logits - top)
    total = jnp.sum(exps, axis=1, keepdims=True)
    first = jnp.sum(exps * logits, axis=1, keepdims=True)
    picked = jnp.sum(jnp.where(matches, logits, 0.0), axis=1, keepdims=True)
    out_ref[:, :PAIR] = jnp.where(matches, -1.0, exps).astype(bf16)
    stats = [top] + two(total) + two(first) + two(picked) + three(inverse) + three(values)
    out_ref[:, PAIR:] = lanes(64, stats).astype(bf16)
    pieces = lanes(64, [top] + two(total) + two(picked)).astype(bf16)
    place = lax.broadcasted_iota(jnp.int32, (64, 128), 0)
    natural = lax.broadcasted_iota(jnp.int32, (64, 128), 1)
    wanted_place = ((natural // 4) % 4) * 16 + (natural // 32) * 4 + natural % 4
    mine = (natural // 16) % 2 == core_ref[0]
    moved = jnp.where((place == wanted_place) & mine, 1.0, 0.0).astype(bf16)
    rows_ref[...] = lax.dot_general(
        pieces, moved, (((0,), (0,)), ((), ())), preferred_element_type=f32
    )[0:16].astype(bf16)


def pull(exps_ref, near_ref, far_ref, rows_ref, got_ref, out_ref, far_held, arrived):
    copies = pieces_of(far_ref, far_held, arrived)
    pieces = [
        exps_ref[s, x * 16 : x * 16 + 16] for x in range(4) for s in range(4)
    ]
    chosen = jnp.concatenate(pieces, axis=0)
    product = wanted = 0.0
    start = 0
    for head in heads_of(near_ref, far_held, copies):
        exps = chosen[:, start : start + head.shape[0]].astype(f32)
        start += head.shape[0]
        product += jnp.dot(
            jnp.maximum(exps, 0.0).astype(bf16), head, preferred_element_type=f32
        )
        wanted += jnp.dot(
            jnp.where(exps < 0.0, 1.0, 0.0).astype(bf16), head, preferred_element_type=f32
        )
    product, wanted = product.astype(bf16), wanted.astype(bf16)
    rows = (rows_ref[...].astype(f32) + got_ref[...].astype(f32)).astype(bf16)
    for x in range(4):
        some = slice(x * 64, x * 64 + 64)
        out_ref[x, :, 0:WIDTH] = product[some]
        out_ref[x, :, WIDTH:STATS] = wanted[some]
        out_ref[x, :, STATS:ROWS] = chosen[some, PAIR:]
        out_ref[x, 0:16, ROWS:] = rows
        out_ref[x, 16:64, ROWS:] = jnp.zeros((48, 128), bf16)


def read_rows(block):
    block = block.astype(f32)
    return block[0:1], block[1:2] + block[2:3], block[3:4] + block[4:5]


def read_lanes(block):
    block = block.astype(f32)
    return take(block, 0, 1), take(block, 1, 3), take(block, 3, 5), take(block, 5, 7)


def merge(pairs):
    top = pairs[0][0]
    for pair in pairs[1:]:
        top = jnp.maximum(top, pair[0])
    weights = [jnp.exp(pair[0] - top) for pair in pairs]
    total = weights[0] * pairs[0][1]
    for weight, pair in zip(weights[1:], pairs[1:]):
        total = total + weight * pair[1]
    return top, weights, total


def join(sources):
    stats = [read_lanes(source[1]) for source in sources]
    top, weights, total = merge(stats)
    first = sum(weight * stat[2] for weight, stat in zip(weights, stats))
    picked = sum(stat[3] for stat in stats)
    product = sum(
        weight * source[0].astype(f32) for weight, source in zip(weights, sources)
    )
    return product, top, total, first, picked


def join_rows(blocks):
    top, _, total = merge(blocks)
    return top, total, sum(block[2] for block in blocks)


def join_x(got_ref, out_ref):
    product, top, total, first, picked = join(
        [(got_ref[k, :, 0:WIDTH], got_ref[k, :, STATS:ROWS]) for k in range(4)]
    )
    top_row, total_row, picked_row = join_rows(
        [read_rows(got_ref[k, 0:16, ROWS:]) for k in range(4)]
    )
    stats = lanes(64, [top] + two(total) + two(first) + two(picked))
    pieces = two(top_row + jnp.log(total_row)) + two(picked_row)
    row = lax.broadcasted_iota(jnp.int32, (4, 128), 0)
    block = jnp.zeros((4, 128), f32)
    for index in range(4):
        block = jnp.where(row == index, pieces[index], block)
    wanted = sum(got_ref[k, :, WIDTH:STATS].astype(f32) for k in range(4))
    for z in range(16):
        some = slice(z * 4, z * 4 + 4)
        out_ref[z, :, 0:WIDTH] = product[some].astype(bf16)
        out_ref[z, :, WIDTH : 2 * WIDTH] = wanted[some].astype(bf16)
        out_ref[z, :, 2 * WIDTH : 2 * WIDTH + 128] = stats[some].astype(bf16)
        out_ref[z, :, ROWS:] = block.astype(bf16)


def finish(
    got_ref, own_ref, hidden_ref, gain_ref, value_ref, token_ref, grad_ref, logprobs_ref
):
    product, top, total, first, picked = join(
        [
            (got_ref[k, :, 0:WIDTH], got_ref[k, :, 2 * WIDTH : 2 * WIDTH + 128])
            for k in range(16)
        ]
    )
    wanted = sum(got_ref[k, :, WIDTH : 2 * WIDTH].astype(f32) for k in range(16))
    log_norm = top + jnp.log(total)
    back = product / total + (jnp.exp(picked - log_norm) - 1.0) * wanted
    own = own_ref[...].astype(f32)
    inverse = take(own, 7, 10)
    values = take(own, 10, 13)
    token = token_ref[...]
    live, weight, value_target = token[:, 0:1], token[:, 1:2], token[:, 2:3]
    value_error = values - value_target
    cotangent = live * (weight * back + value_error * value_ref[...])
    inner = live * (weight * (first / total - picked) + value_error * values)
    rows = hidden_ref[...].astype(f32)
    grad_ref[...] = (
        inverse * gain_ref[...] * cotangent - rows * (inverse * inverse * inner / FULL)
    ).astype(bf16)
    blocks = []
    for k in range(16):
        block = got_ref[k, :, ROWS:].astype(f32)
        blocks.append((block[0:1] + block[1:2], 1.0, block[2:3] + block[3:4]))
    top_row, total_row, picked_row = join_rows(blocks)
    logprobs_ref[...] = picked_row - (top_row + jnp.log(total_row))


def shards(
    hidden, norm_gain, value_weight, head_weight, targets, response_mask, loss_weight, value_target
):
    core = lax.axis_index("core")
    z, x = lax.axis_index("z"), lax.axis_index("x")
    near = (z * 2 + core) * 4 + x
    far = (z * 2 + 1 - core) * 4 + x
    gain, value_row = norm_gain[None, :], value_weight[None, :]
    swap = [(0, 1), (1, 0)]

    copies, head_late = lax.optimization_barrier(
        (jnp.broadcast_to(hidden[None], (16,) + hidden.shape), head_weight)
    )
    half = VOCAB // 2
    upper = lax.ppermute(head_late[:half], "core", swap)
    lower = lax.ppermute(head_late[half:], "core", swap)
    far_weight = pl.pallas_call(
        park,
        out_shape=jax.ShapeDtypeStruct((PARKED, WIDTH), bf16),
        in_specs=[pl.BlockSpec(memory_space=pltpu.VMEM)] * 2,
        out_specs=pl.BlockSpec(memory_space=pl.ANY),
        scratch_shapes=[pltpu.SemaphoreType.DMA((2,))],
        compiler_params=pltpu.CompilerParams(vmem_limit_bytes=SCOPED),
    )(upper, lower)
    by_z = lax.all_to_all(copies, "z", 0, 0)
    block = targets.reshape(4, 2, 4, 4).transpose(1, 2, 0, 3).reshape(2, 64)
    block = jnp.where(core == 0, block[0], block[1])
    in_near, in_far = block - near * VOCAB, block - far * VOCAB
    place = jnp.where((in_near >= 0) & (in_near < VOCAB), in_near, -1)
    place = jnp.where((in_far >= 0) & (in_far < VOCAB), in_far + VOCAB, place)
    place = place.reshape(64, 1)
    by_z, far_weight, place = lax.optimization_barrier((by_z, far_weight, place))
    own = lax.all_gather(by_z.reshape(64, WIDTH), "x", axis=0, tiled=True)
    (sent,) = call(
        project,
        [((4, 64, CODED), jnp.int16)],
        own,
        gain,
        value_row,
        head_weight,
        far_weight,
        parked=4,
    )
    parts = lax.all_to_all(sent, "section", 0, 0)

    exps, rows = pl.pallas_call(
        soften,
        out_shape=[
            jax.ShapeDtypeStruct((64, CODED), bf16),
            jax.ShapeDtypeStruct((16, 128), bf16),
        ],
        in_specs=[
            pl.BlockSpec(memory_space=pltpu.SMEM),
            pl.BlockSpec(memory_space=pltpu.VMEM),
            pl.BlockSpec(memory_space=pltpu.VMEM),
        ],
        compiler_params=pltpu.CompilerParams(vmem_limit_bytes=SCOPED),
    )(core.astype(jnp.int32).reshape(1), parts, place)
    got_rows = lax.ppermute(rows, "core", swap)
    every = lax.all_gather(exps, "section", axis=0)
    (sent,) = call(
        pull,
        [((4, 64, ROWS + 128), bf16)],
        every,
        head_weight,
        far_weight,
        rows,
        got_rows,
        parked=2,
    )
    own_stats = lax.dynamic_slice(every, (z // 4, x * 16 + (z % 4) * 4, PAIR), (1, 4, 128))[0]
    got = lax.all_to_all(sent, "x", 0, 0)
    (sent,) = call(join_x, [((16, 4, ROWS + 128), bf16)], got)
    got = lax.all_to_all(sent, "z", 0, 0)
    token = jnp.stack([response_mask.astype(f32), loss_weight, value_target], axis=1)
    grad, logprobs = call(
        finish,
        [((4, WIDTH), bf16), ((1, 128), f32)],
        got,
        own_stats,
        hidden,
        gain,
        value_row,
        token,
    )
    values = jnp.sum(own_stats[:, 10:13].astype(f32), axis=1)
    return (logprobs.reshape(128), values, grad)


def solution(mesh):
    fine = jax.sharding.Mesh(
        mesh.devices.reshape(4, 16, 2, 4), ("section", "z", "core", "x")
    )
    group = ("z", "core", "x")
    in_specs = (
        P(group, "section"),
        P("section"),
        P("section"),
        P(group, "section"),
        P("section"),
        P(group),
        P(group),
        P(group),
    )
    out_specs = (P("section"), P(group), P(group, "section"))
    return jax.shard_map(shards, mesh=fine, in_specs=in_specs, out_specs=out_specs, check_vma=False)
```
